512 devices in a mesh: src: 16 (over x, y_hi, core), tgt: 32 (over y_lo, z).
Axes of the slice: x: 4, y: 8 (y_hi: 2, y_lo: 4; y = y_hi * 4 + y_lo), z: 8, core: 2. Of those that a mesh axis runs over, the one named last changes fastest.
Arguments:
- coefficients: bfloat16 [16, 32, 512, 512], P('src', 'tgt'), may hold values from -6 to 6
- transfer_blocks: bfloat16 [4, 16, 32, 512, 1024], P(None, 'src', 'tgt'), may hold values from -0.1875 to 0.1875
Outputs:
- result: bfloat16 [16, 32, 512, 512], P('src', 'tgt')
The draws below stay inside these ranges and needn't reach their ends.
All inputs are finite; a program needn't handle non-finite values.
Results may differ from the reference program's by a relative error of at most 0.0064.
Values may be sent and summed in bfloat16 or wider, within the bound.
A program may use at most 64 MiB of HBM per device.

```python
import jax
import jax.numpy as jnp
from jax import lax

RANK = 512
COLS = 512
LEVELS = 4
N_SRC = 16
N_TGT = 32


def steps_of(rng, shape, shards, smallest, top_value):
    gain = 1.0
    for dim, shards_of in shards:
        steps = jax.random.uniform(jax.random.fold_in(jax.random.fold_in(rng, 6), dim), (shards_of,), jnp.float32, smallest / len(shards), top_value / len(shards))
        gain = gain * jnp.repeat(jnp.exp(steps), shape[dim] // shards_of).reshape((-1,) + (1,) * (len(shape) - 1 - dim))
    return gain


def scatter_about(stream_key, shape, scale, most, shards=(), kind=jnp.bfloat16):
    entries = jax.random.normal(stream_key, shape, jnp.float32) * scale
    if len(shards) > 0:
        entries = steps_of(stream_key, shape, shards, -0.22, 0.18) * entries
    return jnp.clip(entries, min=-most, max=most).astype(kind)


def setup_inputs(seed: int = 0) -> dict:
    streams_of = jax.random.split(jax.random.key(seed), 3)
    return {
        "coefficients": scatter_about(streams_of[0], (N_SRC, N_TGT, RANK, COLS), 1.0, 6.0, ((0, 16), (1, 32))),
        "transfer_blocks": scatter_about(streams_of[1], (LEVELS, N_SRC, N_TGT, RANK, 2 * RANK), (2 * RANK) ** -0.5, 0.1875, ((1, 16), (2, 32))),
    }


def level(current, blocks, axis, bit):
    length = current.shape[axis]
    indices = jnp.arange(length, dtype=jnp.int32)
    low_index = (indices & (~(1 << bit))).astype(jnp.int32)
    high_index = (indices | (1 << bit)).astype(jnp.int32)
    low_half = jnp.take(current, low_index, axis=axis)
    high_half = jnp.take(current, high_index, axis=axis)
    stacked = jnp.concatenate([low_half, high_half], axis=2)

    def apply_group(operand_pair):
        block_now, stack_now = operand_pair
        product = jnp.einsum("tij,tjc->tic", block_now.astype(jnp.float32), stack_now.astype(jnp.float32))
        return product.astype(jnp.bfloat16)

    return lax.map(apply_group, (blocks, stacked))


def reference(coefficients, transfer_blocks):
    src_top = N_SRC.bit_length() - 2
    tgt_top = N_TGT.bit_length() - 2
    slab_rows = RANK // N_TGT
    current = level(coefficients, transfer_blocks[0], 0, 0)
    current = level(current, transfer_blocks[1], 0, src_top)
    current = current.reshape(N_SRC, N_TGT, N_TGT, slab_rows, COLS)
    current = current.transpose(0, 2, 1, 3, 4).reshape(N_SRC, N_TGT, RANK, COLS)
    current = level(current, transfer_blocks[2], 1, tgt_top)
    current = level(current, transfer_blocks[3], 1, 0)
    return current
```

```python
import functools

import jax
import jax.numpy as jnp
from jax import lax
from jax.experimental import pallas as pl
from jax.experimental.pallas import tpu as pltpu
from jax.sharding import PartitionSpec as P

LANES = 128
RUNS = 4
GROUPS = 2
VMEM_MIB = 53
MODES = ("yy", "zz", "zz", "zz")
DEPTH = 2
ORDER = (
    "A0", "A1", "A2", "A3", "B0", "S0", "B1", "Z", "S1", "B2", "S2", "B3", "S3",
    "C10", "Y0", "C20", "C11", "C30", "C21", "D1", "C31", "D0", "E1", "D2", "E0", "D3", "E2", "E3",
)


def kernel(shape, coef, blocks, out, s0, s1, t1, v, w, r, s3, bv,
           load_sem, block_sem, send0, recv0, send1, recv1,
           send_y, recv_y, send_z, recv_z, send3, recv3, near_sem, far_sem):
    n_src, n_tgt, rank, chunks = shape
    nz = n_tgt // RUNS
    slab = rank // n_tgt
    in_group = nz // GROUPS
    src_top = n_src.bit_length() - 2
    src, tgt = lax.axis_index("src"), lax.axis_index("tgt")
    core = lax.rem(src, 2)
    jy, jz = tgt // nz, lax.rem(tgt, nz)
    up0 = pl.multiple_of(core * rank, rank)
    up1 = pl.multiple_of(lax.rem(src // (1 << src_top), 2) * rank, rank)
    up3 = pl.multiple_of(lax.rem(tgt, 2) * rank, rank)
    par = lax.rem(jy, 2)

    def flip(i, bit):
        return i + (1 << bit) * (1 - 2 * lax.rem(i // (1 << bit), 2))

    def y_place(d):
        return lax.rem(jy + d, RUNS) * nz + jz

    def z_place(d):
        return jy * nz + lax.rem(jz + d, nz)

    def signal(sem, peer_src, peer_tgt):
        pl.semaphore_signal(sem, inc=1, device_id={"src": peer_src, "tgt": peer_tgt},
                            device_id_type=pl.DeviceIdType.MESH)

    core_src, x_src = flip(src, 0), flip(src, src_top)

    barrier = pltpu.get_barrier_semaphore()
    signal(barrier, x_src - core, tgt)

    @pl.when(core == 1)
    def _():
        signal(barrier, core_src, tgt)

    for d in range(1, RUNS):
        signal(barrier, src - core, y_place(d))
    for d in range(1, nz):
        signal(barrier, src - core + 1, z_place(d))

    loads = []
    for c in range(chunks):
        loads.append(pltpu.make_async_copy(
            coef.at[0, 0, :, pl.ds(c * LANES, LANES)], s0.at[c, pl.ds(up0, rank)], load_sem.at[c]))
        loads[-1].start()
    block_loads = []
    for level in range(4):
        block_loads.append(pltpu.make_async_copy(blocks.at[level, 0, 0], bv.at[level], block_sem.at[level]))
        block_loads[-1].start()

    @pl.when(core == 0)
    def _():
        pl.semaphore_wait(barrier, 3 + 2 * (RUNS - 1))
        signal(near_sem, core_src, tgt)

    @pl.when(core == 1)
    def _():
        pl.semaphore_wait(near_sem, 1)

    def meet_far():
        @pl.when(core == 1)
        def _():
            pl.semaphore_wait(barrier, 2 * (nz - 1))
            signal(far_sem, core_src, tgt)

        @pl.when(core == 0)
        def _():
            pl.semaphore_wait(far_sem, 1)

    def remote(source, target, send, recv, peer_src, peer_tgt):
        return pltpu.make_async_remote_copy(
            src_ref=source, dst_ref=target, send_sem=send, recv_sem=recv,
            device_id={"src": peer_src, "tgt": peer_tgt}, device_id_type=pl.DeviceIdType.MESH)

    def same(buf, c, offset, send, recv, peer_src, peer_tgt):
        ref = buf.at[c, pl.ds(offset, rank)]
        return remote(ref, ref, send.at[c], recv.at[c], peer_src, peer_tgt)

    copies0 = [same(s0, c, up0, send0, recv0, core_src, tgt) for c in range(chunks)]
    copies1 = [same(s1, c, up1, send1, recv1, x_src, tgt) for c in range(chunks)]
    copies3 = [same(s3, c, up3, send3, recv3, src, flip(tgt, 0)) for c in range(chunks)]

    mine = jz // in_group

    def modes(c, way):
        return [g for g in range(GROUPS) if MODES[c][g] == way]

    def among(c, way):
        groups = modes(c, way)
        if len(groups) == GROUPS:
            return lambda f: f()
        if not groups:
            return lambda f: None
        return pl.when(mine == groups[0])

    def members(g):
        return pl.ds(g * in_group, in_group)

    def y_first(c):
        return [remote(t1.at[c, :, lax.rem(par + d, 2)], v.at[c, :, jy], send_y.at[c, mine, d - 1],
                       recv_y.at[c, mine, d - 1], src, y_place(d)) for d in (2, 1, 3)]

    def y_second(c, g):
        return [remote(w.at[c, lax.rem(par + d, 2), members(g)], r.at[c, jy, members(g)],
                       send_y.at[c, g, d - 1], recv_y.at[c, g, d - 1], src, y_place(d)) for d in (2, 1, 3)]

    def z_copies(c, first):
        copies = []
        for d in sorted(range(1, nz), key=lambda d: -min(d, nz - d)):
            there = lax.rem(jz + d, nz)
            source, target = (t1, w) if first else (v, r)
            source, target = source.at[c, there], target.at[c, :, jz]
            copies.append(remote(source, target, send_z.at[c, d - 1], recv_z.at[c, jz], src, z_place(d)))
        return copies

    def wait_z(c, g):
        for z in range(g * in_group, (g + 1) * in_group):
            buf = r if MODES[c][g] == "y" else w
            target = buf.at[c, :, z]

            @pl.when(jz != z)
            def _():
                remote(target, target, send_z.at[c, 0], recv_z.at[c, z], src, z_place(1)).wait_recv()

    def apply(level, stack):
        return jnp.dot(bv[level], stack, preferred_element_type=jnp.float32).astype(jnp.bfloat16)

    for c in range(chunks):
        loads[c].wait()
        copies0[c].start()

    under_way = []

    def finish_y(most):
        while len(under_way) > most:
            under_way.pop(0)()

    def wait_y_first(c):
        @among(c, "y")
        def _():
            for copy in y_first(c):
                copy.wait_send()

    def wait_y_second(c, g):
        for copy in y_second(c, g):
            copy.wait_send()

    for at, step in enumerate(ORDER):
        if step == "Z":
            meet_far()
            continue
        kind, c = step[0], int(step[1])
        if c >= chunks:
            continue
        if kind == "A":
            if c == 0:
                block_loads[0].wait()
            copies0[c].wait_recv()
            s1[c, pl.ds(up1, rank)] = apply(0, s0[c])
            copies1[c].start()
        elif kind == "B":
            if c == 0:
                block_loads[1].wait()
            copies1[c].wait_recv()
            second = apply(1, s1[c]).reshape(2, 2, nz, slab, LANES)
            for half in range(2):
                for p in range(2):
                    t1[c, :, p, half] = second[half, p]
        elif kind == "S":
            if modes(c, "y"):
                finish_y(DEPTH - 1)
                under_way.append(functools.partial(wait_y_first, c))

            @among(c, "y")
            def _():
                for copy in y_first(c):
                    copy.start()
                v[c, :, jy] = t1[c, :, par]

            @among(c, "z")
            def _():
                for copy in z_copies(c, True):
                    copy.start()
                w[c, :, jz] = t1[c, jz]
        elif kind == "Y":
            @among(c, "y")
            def _():
                for copy in y_first(c):
                    copy.wait_recv()
                for copy in z_copies(c, False):
                    copy.start()
                r[c, :, jz] = v[c, jz]
        elif kind == "C":
            g = int(step[2])
            wait_z(c, g)
            finish_y(DEPTH - 1)
            under_way.append(functools.partial(wait_y_second, c, g))
            for copy in y_second(c, g):
                copy.start()
            r[c, jy, members(g)] = w[c, par, members(g)]
        elif kind == "D":
            if not any(e[0] == "D" for e in ORDER[:at]):
                block_loads[2].wait()
            for g in range(GROUPS):
                if MODES[c][g] == "y":
                    wait_z(c, g)
                else:
                    for copy in y_second(c, g):
                        copy.wait_recv()
            stack = [r[c, :, :, half].reshape(rank, LANES) for half in range(2)]
            s3[c, pl.ds(up3, rank)] = apply(2, jnp.concatenate(stack, axis=0))
            copies3[c].start()
        else:
            if not any(e[0] == "E" for e in ORDER[:at]):
                block_loads[3].wait()
            copies3[c].wait_recv()
            out[0, 0, :, pl.ds(c * LANES, LANES)] = apply(3, s3[c])

    finish_y(0)
    for c in range(chunks):
        for copy in [copies0[c], copies1[c], copies3[c]]:
            copy.wait_send()

        @among(c, "y")
        def _():
            for copy in z_copies(c, False):
                copy.wait_send()

        @among(c, "z")
        def _():
            for copy in z_copies(c, True):
                copy.wait_send()


def shards(coefficients, transfer_blocks):
    rank, columns = coefficients.shape[2:]
    chunks = columns // LANES
    n_src, n_tgt = lax.axis_size("src"), lax.axis_size("tgt")
    slab = rank // n_tgt
    nz = n_tgt // RUNS
    kind = jnp.bfloat16
    dma = pltpu.SemaphoreType.DMA
    return pl.pallas_call(
        functools.partial(kernel, (n_src, n_tgt, rank, chunks)),
        out_shape=jax.ShapeDtypeStruct(coefficients.shape, kind),
        in_specs=[pl.BlockSpec(memory_space=pltpu.HBM)] * 2,
        out_specs=pl.BlockSpec(memory_space=pltpu.VMEM),
        scratch_shapes=[
            pltpu.VMEM((chunks, 2 * rank, LANES), kind),
            pltpu.VMEM((chunks, 2 * rank, LANES), kind),
            pltpu.VMEM((chunks, nz, 2, 2, slab, LANES), kind),
            pltpu.VMEM((chunks, nz, RUNS, 2, slab, LANES), kind),
            pltpu.VMEM((chunks, 2, nz, 2, slab, LANES), kind),
            pltpu.VMEM((chunks, RUNS, nz, 2, slab, LANES), kind),
            pltpu.VMEM((chunks, 2 * rank, LANES), kind),
            pltpu.VMEM((4, rank, 2 * rank), kind),
            dma((chunks,)), dma((4,)),
            dma((chunks,)), dma((chunks,)), dma((chunks,)), dma((chunks,)),
            dma((chunks, GROUPS, RUNS - 1)), dma((chunks, GROUPS, RUNS - 1)),
            dma((chunks, nz - 1)), dma((chunks, nz)),
            dma((chunks,)), dma((chunks,)),
            pltpu.SemaphoreType.REGULAR, pltpu.SemaphoreType.REGULAR,
        ],
        compiler_params=pltpu.CompilerParams(
            collective_id=0, has_side_effects=True, vmem_limit_bytes=VMEM_MIB * 2**20),
        cost_estimate=pl.CostEstimate(
            flops=4 * 2 * rank * 2 * rank * columns, bytes_accessed=6 * 2**20, transcendentals=0),
    )(coefficients, transfer_blocks)


def solution(mesh):
    return jax.shard_map(
        shards,
        mesh=mesh,
        in_specs=(P("src", "tgt", None, None), P(None, "src", "tgt", None, None)),
        out_specs=P("src", "tgt", None, None),
        check_vma=False,
    )
```

```python
import functools

import jax
import jax.numpy as jnp
from jax import lax
from jax.experimental import pallas as pl
from jax.experimental.pallas import tpu as pltpu
from jax.sharding import PartitionSpec as P

LANES = 128
RUNS = 4
GROUPS = 4
VMEM_MIB = 53
MODES = ("yyzz", "zzzz", "zzzz", "zzzz")
DEPTH = 4
PIECES = 2
ORDER = (
    "A0", "A1", "A2", "A3", "B0", "Z1", "S0", "B1", "Z0", "S1", "B2", "S2", "C10", "C11", "B3", "S3", "Y0", "C20", "C21",
    "C02", "C03", "C12", "C13", "D0", "C22", "C23", "C30", "C31", "D1", "C32", "C33", "D2", "E0", "D3", "E1", "E2", "E3",
)


def kernel(shape, coef, blocks, out, s0, s1, t1, v, w, r, s3, bv,
           load_sem, block_sem, send0, recv0, send1, recv1,
           send_y, recv_y, send_z, recv_z, send3, recv3, near_sem, far_sem):
    n_src, n_tgt, rank, chunks = shape
    nz = n_tgt // RUNS
    slab = rank // n_tgt
    in_group = nz // GROUPS
    src_top = n_src.bit_length() - 2
    src, tgt = lax.axis_index("src"), lax.axis_index("tgt")
    core = lax.rem(src, 2)
    jy, jz = tgt // nz, lax.rem(tgt, nz)
    up0 = pl.multiple_of(core * rank, rank)
    up1 = pl.multiple_of(lax.rem(src // (1 << src_top), 2) * rank, rank)
    up3 = pl.multiple_of(lax.rem(tgt, 2) * rank, rank)
    par = lax.rem(jy, 2)

    def flip(i, bit):
        return i + (1 << bit) * (1 - 2 * lax.rem(i // (1 << bit), 2))

    def y_place(d):
        return lax.rem(jy + d, RUNS) * nz + jz

    def z_place(d):
        return jy * nz + lax.rem(jz + d, nz)

    def signal(sem, peer_src, peer_tgt):
        pl.semaphore_signal(sem, inc=1, device_id={"src": peer_src, "tgt": peer_tgt},
                            device_id_type=pl.DeviceIdType.MESH)

    core_src, x_src = flip(src, 0), flip(src, src_top)

    barrier = pltpu.get_barrier_semaphore()
    signal(barrier, x_src - core, tgt)

    @pl.when(core == 1)
    def _():
        signal(barrier, core_src, tgt)

    for d in range(1, RUNS):
        signal(barrier, src - core, y_place(d))
    for d in range(1, nz):
        signal(barrier, src - core + 1, z_place(d))

    loads = []
    for c in range(chunks):
        loads.append(pltpu.make_async_copy(
            coef.at[0, 0, :, pl.ds(c * LANES, LANES)], s0.at[c, pl.ds(up0, rank)], load_sem.at[c]))
        loads[-1].start()
    block_loads = []
    for level in range(4):
        block_loads.append(pltpu.make_async_copy(blocks.at[level, 0, 0], bv.at[level], block_sem.at[level]))
        block_loads[-1].start()

    @pl.when(core == 0)
    def _():
        pl.semaphore_wait(barrier, 3 + 2 * (RUNS - 1))
        signal(near_sem, core_src, tgt)

    @pl.when(core == 1)
    def _():
        pl.semaphore_wait(near_sem, 1)

    def meet_far():
        @pl.when(core == 1)
        def _():
            pl.semaphore_wait(barrier, 2 * (nz - 1))
            signal(far_sem, core_src, tgt)

        @pl.when(core == 0)
        def _():
            pl.semaphore_wait(far_sem, 1)

    def remote(source, target, send, recv, peer_src, peer_tgt):
        return pltpu.make_async_remote_copy(
            src_ref=source, dst_ref=target, send_sem=send, recv_sem=recv,
            device_id={"src": peer_src, "tgt": peer_tgt}, device_id_type=pl.DeviceIdType.MESH)

    piece = rank // PIECES

    def same(buf, c, offset, send, recv, peer_src, peer_tgt):
        copies = []
        for p in range(PIECES):
            ref = buf.at[c, pl.ds(pl.multiple_of(offset + p * piece, piece), piece)]
            copies.append(remote(ref, ref, send.at[c, p], recv.at[c, p], peer_src, peer_tgt))
        return copies

    copies0 = [remote(s0.at[c, pl.ds(up0, rank)], s0.at[c, pl.ds(up0, rank)], send0.at[c], recv0.at[c], core_src, tgt)
               for c in range(chunks)]
    copies1 = [same(s1, c, up1, send1, recv1, x_src, tgt) for c in range(chunks)]
    copies3 = [same(s3, c, up3, send3, recv3, src, flip(tgt, 0)) for c in range(chunks)]

    mine = jz // in_group

    def modes(c, way):
        return [g for g in range(GROUPS) if MODES[c][g] == way]

    def among(c, way):
        groups = modes(c, way)
        if len(groups) == GROUPS:
            return lambda f: f()
        if not groups:
            return lambda f: None
        return pl.when(functools.reduce(jnp.logical_or, [mine == g for g in groups]))

    def members(g):
        return pl.ds(g * in_group, in_group)

    def y_first(c):
        return [remote(t1.at[c, :, lax.rem(par + d, 2)], v.at[c, :, jy], send_y.at[c, mine, d - 1],
                       recv_y.at[c, mine, d - 1], src, y_place(d)) for d in (2, 1, 3)]

    def y_second(c, g):
        return [remote(w.at[c, lax.rem(par + d, 2), members(g)], r.at[c, jy, members(g)],
                       send_y.at[c, g, d - 1], recv_y.at[c, g, d - 1], src, y_place(d)) for d in (2, 1, 3)]

    def each_z(c, first, act):
        for z in range(nz):
            source, target = (t1, w) if first else (v, r)
            source, target = source.at[c, z], target.at[c, :, jz]

            @pl.when(jz != z)
            def _():
                act(remote(source, target, send_z.at[c, z], recv_z.at[c, jz], src, jy * nz + z))

    def wait_z(c, g):
        for z in range(g * in_group, (g + 1) * in_group):
            buf = r if MODES[c][g] == "y" else w
            target = buf.at[c, :, z]

            @pl.when(jz != z)
            def _():
                remote(target, target, send_z.at[c, z], recv_z.at[c, z], src, jy * nz + z).wait_recv()

    def dot(a, b):
        return jnp.dot(a, b, preferred_element_type=jnp.float32)

    def receive(level, buf, c, arrivals):
        for copy in arrivals:
            copy.wait_recv()
        return dot(bv[level], buf[c]).astype(jnp.bfloat16)

    def send_pieces(buf, c, offset, copies, make):
        for p, copy in enumerate(copies):
            buf[c, pl.ds(pl.multiple_of(offset + p * piece, piece), piece)] = make(p * piece)
            copy.start()

    for c in range(chunks):
        loads[c].wait()
        copies0[c].start()

    under_way = []

    def finish_y(most):
        while len(under_way) > most:
            under_way.pop(0)()

    def wait_y_first(c):
        @among(c, "y")
        def _():
            for copy in y_first(c):
                copy.wait_send()

    def wait_y_second(c, g):
        for copy in y_second(c, g):
            copy.wait_send()

    for at, step in enumerate(ORDER):
        if step[0] == "Z":
            pl.when(mine // (GROUPS // 2) == int(step[1]))(meet_far)
            continue
        kind, c = step[0], int(step[1])
        if c >= chunks:
            continue
        if kind == "A":
            if c == 0:
                block_loads[0].wait()
            first = receive(0, s0, c, [copies0[c]])
            send_pieces(s1, c, up1, copies1[c], lambda row: first[row:row + piece])
        elif kind == "B":
            if c == 0:
                block_loads[1].wait()
            second = receive(1, s1, c, copies1[c]).reshape(2, 2, nz, slab, LANES)
            for half in range(2):
                for p in range(2):
                    t1[c, :, p, half] = second[half, p]
        elif kind == "S":
            if modes(c, "y"):
                finish_y(DEPTH - 1)
                under_way.append(functools.partial(wait_y_first, c))

            @among(c, "y")
            def _():
                for copy in y_first(c):
                    copy.start()
                v[c, :, jy] = t1[c, :, par]

            @among(c, "z")
            def _():
                each_z(c, True, lambda copy: copy.start())
                w[c, :, jz] = t1[c, jz]
        elif kind == "Y":
            @among(c, "y")
            def _():
                for copy in y_first(c):
                    copy.wait_recv()
                each_z(c, False, lambda copy: copy.start())
                r[c, :, jz] = v[c, jz]
        elif kind == "C":
            g = int(step[2])
            wait_z(c, g)
            finish_y(DEPTH - 1)
            under_way.append(functools.partial(wait_y_second, c, g))
            for copy in y_second(c, g):
                copy.start()
            r[c, jy, members(g)] = w[c, par, members(g)]
        elif kind == "D":
            if not any(e[0] == "D" for e in ORDER[:at]):
                block_loads[2].wait()
            for g in range(GROUPS):
                if MODES[c][g] == "y":
                    wait_z(c, g)
                else:
                    for copy in y_second(c, g):
                        copy.wait_recv()
            stack = [r[c, :, :, half].reshape(rank, LANES) for half in range(2)]
            stack = jnp.concatenate(stack, axis=0)
            send_pieces(s3, c, up3, copies3[c],
                        lambda row: dot(bv[2, row:row + piece], stack).astype(jnp.bfloat16))
        else:
            if not any(e[0] == "E" for e in ORDER[:at]):
                block_loads[3].wait()
            out[0, 0, :, pl.ds(c * LANES, LANES)] = receive(3, s3, c, copies3[c])

    finish_y(0)
    for c in range(chunks):
        for copy in [copies0[c]] + copies1[c] + copies3[c]:
            copy.wait_send()

        @among(c, "y")
        def _():
            each_z(c, False, lambda copy: copy.wait_send())

        @among(c, "z")
        def _():
            each_z(c, True, lambda copy: copy.wait_send())


def shards(coefficients, transfer_blocks):
    rank, columns = coefficients.shape[2:]
    chunks = columns // LANES
    n_src, n_tgt = lax.axis_size("src"), lax.axis_size("tgt")
    slab = rank // n_tgt
    nz = n_tgt // RUNS
    kind = jnp.bfloat16
    dma = pltpu.SemaphoreType.DMA
    return pl.pallas_call(
        functools.partial(kernel, (n_src, n_tgt, rank, chunks)),
        out_shape=jax.ShapeDtypeStruct(coefficients.shape, kind),
        in_specs=[pl.BlockSpec(memory_space=pltpu.HBM)] * 2,
        out_specs=pl.BlockSpec(memory_space=pltpu.VMEM),
        scratch_shapes=[
            pltpu.VMEM((chunks, 2 * rank, LANES), kind),
            pltpu.VMEM((chunks, 2 * rank, LANES), kind),
            pltpu.VMEM((chunks, nz, 2, 2, slab, LANES), kind),
            pltpu.VMEM((chunks, nz, RUNS, 2, slab, LANES), kind),
            pltpu.VMEM((chunks, 2, nz, 2, slab, LANES), kind),
            pltpu.VMEM((chunks, RUNS, nz, 2, slab, LANES), kind),
            pltpu.VMEM((chunks, 2 * rank, LANES), kind),
            pltpu.VMEM((4, rank, 2 * rank), kind),
            dma((chunks,)), dma((4,)),
            dma((chunks,)), dma((chunks,)), dma((chunks, PIECES)), dma((chunks, PIECES)),
            dma((chunks, GROUPS, RUNS - 1)), dma((chunks, GROUPS, RUNS - 1)),
            dma((chunks, nz)), dma((chunks, nz)),
            dma((chunks, PIECES)), dma((chunks, PIECES)),
            pltpu.SemaphoreType.REGULAR, pltpu.SemaphoreType.REGULAR,
        ],
        compiler_params=pltpu.CompilerParams(
            collective_id=0, has_side_effects=True, vmem_limit_bytes=VMEM_MIB * 2**20),
        cost_estimate=pl.CostEstimate(
            flops=4 * 2 * rank * 2 * rank * columns, bytes_accessed=6 * 2**20, transcendentals=0),
    )(coefficients, transfer_blocks)


def solution(mesh):
    return jax.shard_map(
        shards,
        mesh=mesh,
        in_specs=(P("src", "tgt", None, None), P(None, "src", "tgt", None, None)),
        out_specs=P("src", "tgt", None, None),
        check_vma=False,
    )
```
